512 devices in a mesh: ex: 32 (over z, x_hi), par: 16 (over y, x_lo, core).
Axes of the slice: x: 4 (x_hi: 2, x_lo: 2; x = x_hi * 2 + x_lo), y: 4, z: 16, core: 2. Of those that a mesh axis runs over, the one named last changes fastest.
Arguments:
- jacobian: bfloat16 [2560, 131072], P('ex', 'par'), may hold values from -0.29882812 to 0.29882812
Outputs:
- gram: float32 [2560, 2560], P('ex', 'par')
The draws below stay inside these ranges and needn't reach their ends.
All inputs are finite; a program needn't handle non-finite values.
Results may differ from the reference program's by a relative error of at most 0.0035.
Values may be sent and summed in bfloat16 or wider, within the bound.
No kernel may reach another device: no remote copies, remote signals or barrier semaphores. Data moves between devices by JAX's collectives and lax.ppermute only.
A program may use at most 64 MiB of HBM per device.

```python
import jax
import jax.numpy as jnp

PARAMS = 131072
ROWS = 2560


def level_of(own_key, extent, pieces, least, top_value):
    def one(dim, blocks):
        heights = jax.random.uniform(jax.random.fold_in(jax.random.fold_in(own_key, 6), dim), (blocks,), jnp.float32, least / len(pieces), top_value / len(pieces))
        return jnp.repeat(jnp.exp(heights), extent[dim] // blocks).reshape((-1,) + (1,) * (len(extent) - dim - 1))

    loudness = one(*pieces[0])
    for cut in pieces[1:]:
        loudness = loudness * one(*cut)
    return loudness


def normal_values(key, shape, spread, reach, cuts=(), held_as=jnp.bfloat16):
    loudness = level_of(key, shape, cuts, -0.22, 0.18) if cuts else 1.0
    drawn = jax.random.normal(key, shape, jnp.float32) * spread * loudness
    return jnp.minimum(jnp.maximum(drawn, -reach), reach).astype(held_as)


def setup_inputs(seed: int = 0) -> dict:
    keys = jax.random.split(jax.random.key(seed), 2)
    return {
        "jacobian": normal_values(keys[0], (ROWS, PARAMS), 0.0525, 0.29882812, ((0, 32), (1, 16))),
    }


def reference(jacobian):
    return jnp.dot(jacobian, jacobian.T, preferred_element_type=jnp.float32)
```

```python
import jax
import jax.numpy as jnp
from jax import lax
from jax.sharding import PartitionSpec as P

CHUNKS = 2
AXES = ("ex", "par")


def tile_of(rows_a, rows_b):
    return lax.dot_general(
        rows_a, rows_b, (((1,), (1,)), ((), ())), preferred_element_type=jnp.float32
    )


def shards(jacobian):
    ex_size, par_size = lax.axis_size("ex"), lax.axis_size("par")
    planes = ex_size // 2
    half = planes // 2
    position, column = lax.axis_index("ex"), lax.axis_index("par")
    plane, member, core = position // 2, position % 2, column % 2
    way = 1 - 2 * core
    rows, cols = jacobian.shape
    pair_cols = cols // 2
    width = pair_cols // CHUNKS
    swap = [(i, i ^ 1) for i in range(ex_size)]
    onward = [
        (i * par_size + p, ((i + (2 if p % 2 == 0 else -2)) % ex_size) * par_size + p)
        for i in range(ex_size)
        for p in range(par_size)
    ]

    def pair_block(index):
        out = lax.dynamic_slice_in_dim(jacobian, (1 - member) * pair_cols + index * width, width, 1)
        got = lax.ppermute(out, "ex", swap)
        mine = lax.dynamic_slice_in_dim(jacobian, member * pair_cols + index * width, width, 1)
        return jnp.where(
            member == 0, jnp.concatenate([mine, got], 0), jnp.concatenate([got, mine], 0)
        )

    own = [pair_block(c) for c in range(CHUNKS)]
    strip = jnp.zeros((2, planes, rows, 2 * rows), jnp.bfloat16)

    def put(strip, tile, where):
        block = tile.astype(jnp.bfloat16).reshape(2, 1, rows, 2 * rows)
        return lax.dynamic_update_slice_in_dim(strip, block, jnp.mod(where, planes), 1)

    strip = put(strip, sum(tile_of(own[c], own[c]) for c in range(CHUNKS)), plane)
    travel = list(own)
    for step in range(1, half):
        for c in range(CHUNKS):
            travel[c] = lax.ppermute(travel[c], AXES, onward)
        tile = sum(tile_of(own[c], travel[c]) for c in range(CHUNKS))
        strip = put(strip, tile, plane - way * step)
    theirs = jnp.mod(plane + way, planes) // half
    got = lax.ppermute(jnp.where(theirs == 0, travel[0], travel[1]), AXES, onward)
    strip = put(strip, tile_of(jnp.where(plane // half == 0, own[0], own[1]), got), plane + half)

    groups = [
        [(2 * z + m) * par_size + p for m in range(2) for p in range(par_size)]
        for z in range(planes)
    ]
    parts = strip.reshape(2 * planes, rows, 2 * rows)
    parts = lax.all_to_all(parts, AXES, 0, 0, axis_index_groups=groups, tiled=True)
    mine = jnp.sum(parts.astype(jnp.float32), axis=0)

    def mirror(across):
        pairs = [
            ((2 * z + m) * par_size + p, (2 * p + (m ^ across)) * par_size + z)
            for z in range(planes)
            for m in range(2)
            for p in range(par_size)
            if p != z
        ]
        block = lax.dynamic_slice_in_dim(mine, (member ^ across) * rows, rows, 1)
        return lax.ppermute(block.T, AXES, pairs)

    same, other = mirror(0), mirror(1)
    added = jnp.where(
        member == 0, jnp.concatenate([same, other], 1), jnp.concatenate([other, same], 1)
    )
    return mine + added


def solution(mesh):
    return jax.shard_map(
        shards, mesh=mesh, in_specs=(P("ex", "par"),), out_specs=P("ex", "par"), check_vma=False
    )
```

```python
import jax
import jax.numpy as jnp
from jax import lax
from jax.sharding import PartitionSpec as P

AXES = ("ex", "par")
CHUNKS = 2
LANES = 128


def tile_of(rows_a, rows_b):
    return lax.dot_general(
        rows_a, rows_b, (((1,), (1,)), ((), ())), preferred_element_type=jnp.float32
    )


def shards(jacobian):
    ex_size, par_size = lax.axis_size("ex"), lax.axis_size("par")
    planes = ex_size // 2
    half = planes // 2
    position, column = lax.axis_index("ex"), lax.axis_index("par")
    plane, member, core = position // 2, position % 2, column % 2
    way = 1 - 2 * core
    rows, cols = jacobian.shape
    width = cols // CHUNKS
    swap = [(i, i ^ 1) for i in range(ex_size)]
    onward = [
        (i * par_size + p, ((i + (2 if p % 2 == 0 else -2)) % ex_size) * par_size + p)
        for i in range(ex_size)
        for p in range(par_size)
    ]

    def in_order(block_a, block_b):
        return jnp.where(
            member == 0,
            jnp.concatenate([block_a, block_b], 0),
            jnp.concatenate([block_b, block_a], 0),
        )

    def hop(block):
        return lax.ppermute(block, AXES, onward)

    strip = jnp.zeros((planes, rows, 2 * rows), jnp.bfloat16)

    def put(strip, travel, held, where):
        tile = sum(tile_of(block, block_held) for block, block_held in zip(travel, held))
        return lax.dynamic_update_slice_in_dim(
            strip, tile.astype(jnp.bfloat16)[None], jnp.mod(where, planes), 0
        )

    mine = [lax.slice_in_dim(jacobian, c * width, (c + 1) * width, axis=1) for c in range(CHUNKS)]
    own = [in_order(block, lax.ppermute(block, "ex", swap)) for block in mine]
    travel = list(mine)
    strip = put(strip, travel, own, plane)
    for step in range(1, half):
        travel = [hop(block) for block in travel]
        strip = put(strip, travel, own, plane - way * step)

    def side_of(block, side):
        return lax.dynamic_slice_in_dim(block, side * (width // 2), width // 2, 1)

    theirs_side = jnp.mod(plane + way, planes) // half
    travel = [hop(side_of(block, theirs_side)) for block in travel]
    held = [side_of(block, plane // half) for block in own]
    strip = put(strip, travel, held, plane + half)

    groups = [[e * par_size + p for p in range(par_size)] for e in range(ex_size)]
    parts = lax.all_to_all(strip, AXES, 0, 0, axis_index_groups=groups, tiled=True)
    total = jnp.sum(parts.astype(jnp.float32), axis=0)
    mirror = [
        ((2 * z + m) * par_size + p, (2 * p + m) * par_size + z)
        for z in range(planes)
        for m in range(2)
        for p in range(par_size)
        if p != z
    ]
    packed = total.reshape(rows * 2 * rows // LANES, LANES)
    added = lax.ppermute(packed, AXES, mirror).reshape(rows, 2 * rows)
    away = lax.dynamic_slice_in_dim(total, (1 - member) * rows, rows, 1)
    kept = lax.dynamic_slice_in_dim(total, member * rows, rows, 1)
    got = lax.ppermute(away, "ex", swap)
    return in_order(kept, got).T + added


def solution(mesh):
    return jax.shard_map(
        shards, mesh=mesh, in_specs=(P("ex", "par"),), out_specs=P("ex", "par"), check_vma=False
    )
```

```python
import jax
import jax.numpy as jnp
from jax import lax
from jax.sharding import PartitionSpec as P

AXES = ("ex", "par")
CHUNKS = 2
LANES = 128


def tile_of(rows_a, rows_b):
    return lax.dot_general(
        rows_a, rows_b, (((1,), (1,)), ((), ())), preferred_element_type=jnp.float32
    )


def shards(jacobian):
    ex_size, par_size = lax.axis_size("ex"), lax.axis_size("par")
    planes = ex_size // 2
    half = planes // 2
    position, column = lax.axis_index("ex"), lax.axis_index("par")
    plane, member, core = position // 2, position % 2, column % 2
    way = 1 - 2 * core
    rows, cols = jacobian.shape
    width = cols // CHUNKS
    swap = [(i, i ^ 1) for i in range(ex_size)]
    onward = [
        (i * par_size + p, ((i + (2 if p % 2 == 0 else -2)) % ex_size) * par_size + p)
        for i in range(ex_size)
        for p in range(par_size)
    ]

    def in_order(block_a, block_b):
        return jnp.where(
            member == 0,
            jnp.concatenate([block_a, block_b], 0),
            jnp.concatenate([block_b, block_a], 0),
        )

    def hop(block):
        return lax.ppermute(block, AXES, onward)

    strip = jnp.zeros((planes, rows, 2 * rows), jnp.bfloat16)

    def put(strip, travel, held, where):
        tile = sum(tile_of(block, block_held) for block, block_held in zip(travel, held))
        return lax.dynamic_update_slice_in_dim(
            strip, tile.astype(jnp.bfloat16)[None], jnp.mod(where, planes), 0
        )

    mine = [lax.slice_in_dim(jacobian, c * width, (c + 1) * width, axis=1) for c in range(CHUNKS)]
    own = [in_order(block, lax.ppermute(block, "ex", swap)) for block in mine]
    travel = list(mine)
    strip = put(strip, travel, own, plane)
    for step in range(1, half):
        travel = [hop(block) for block in travel]
        strip = put(strip, travel, own, plane - way * step)

    def side_of(block, side):
        return lax.dynamic_slice_in_dim(block, side * (width // 2), width // 2, 1)

    theirs_side = jnp.mod(plane + way, planes) // half
    travel = [hop(side_of(block, theirs_side)) for block in travel]
    held = [side_of(block, plane // half) for block in own]
    strip = put(strip, travel, held, plane + half)

    groups = [[e * par_size + p for p in range(par_size)] for e in range(ex_size)]
    parts = lax.all_to_all(strip, AXES, 0, 0, axis_index_groups=groups, tiled=True)
    total = jnp.sum(parts.astype(jnp.float32), axis=0)
    mirror = [
        ((2 * z + m) * par_size + p, (2 * p + m) * par_size + z)
        for z in range(planes)
        for m in range(2)
        for p in range(par_size)
        if p != z
    ]
    added = lax.ppermute(total, AXES, mirror)
    away = lax.dynamic_slice_in_dim(total, (1 - member) * rows, rows, 1)
    kept = lax.dynamic_slice_in_dim(total, member * rows, rows, 1)
    got = lax.ppermute(away, "ex", swap)
    return in_order(kept, got).T + added


def solution(mesh):
    return jax.shard_map(
        shards, mesh=mesh, in_specs=(P("ex", "par"),), out_specs=P("ex", "par"), check_vma=False
    )
```

```python
import jax
import jax.numpy as jnp
from jax import lax
from jax.sharding import PartitionSpec as P

AXES = ("ex", "par")
CHUNKS = 2
LANES = 128


def tile_of(rows_a, rows_b):
    return lax.dot_general(
        rows_a, rows_b, (((1,), (1,)), ((), ())), preferred_element_type=jnp.float32
    )


def shards(jacobian):
    ex_size, par_size = lax.axis_size("ex"), lax.axis_size("par")
    planes = ex_size // 2
    half = planes // 2
    position, column = lax.axis_index("ex"), lax.axis_index("par")
    plane, member, core = position // 2, position % 2, column % 2
    way = 1 - 2 * core
    rows, cols = jacobian.shape
    width = cols // CHUNKS
    swap = [(i, i ^ 1) for i in range(ex_size)]
    onward = [
        (i * par_size + p, ((i + (2 if p % 2 == 0 else -2)) % ex_size) * par_size + p)
        for i in range(ex_size)
        for p in range(par_size)
    ]

    def in_order(block_a, block_b):
        return jnp.where(
            member == 0,
            jnp.concatenate([block_a, block_b], 0),
            jnp.concatenate([block_b, block_a], 0),
        )

    def hop(block):
        return lax.ppermute(block, AXES, onward)

    strip = jnp.zeros((planes, rows, 2 * rows), jnp.bfloat16)

    def slot_of(place):
        return place % 2 * (par_size // 2) + place // 2

    def put(strip, travel, held, where):
        tile = sum(tile_of(block, block_held) for block, block_held in zip(travel, held))
        return lax.dynamic_update_slice_in_dim(
            strip, tile.astype(jnp.bfloat16)[None], slot_of(jnp.mod(where, planes)), 0
        )

    mine = [lax.slice_in_dim(jacobian, c * width, (c + 1) * width, axis=1) for c in range(CHUNKS)]
    own = [in_order(block, lax.ppermute(block, "ex", swap)) for block in mine]
    travel = list(mine)
    strip = put(strip, travel, own, plane)
    for step in range(1, half):
        travel = [hop(block) for block in travel]
        strip = put(strip, travel, own, plane - way * step)

    def side_of(block, side):
        return lax.dynamic_slice_in_dim(block, side * (width // 2), width // 2, 1)

    theirs_side = jnp.mod(plane + way, planes) // half
    travel = [hop(side_of(block, theirs_side)) for block in travel]
    held = [side_of(block, plane // half) for block in own]
    strip = put(strip, travel, held, plane + half)

    by_slot = sorted(range(par_size), key=slot_of)
    groups = [[e * par_size + p for p in by_slot] for e in range(ex_size)]
    parts = lax.all_to_all(strip, AXES, 0, 0, axis_index_groups=groups, tiled=True)
    total = jnp.sum(parts.astype(jnp.float32), axis=0)
    mirror = [
        ((2 * z + m) * par_size + p, (2 * p + m) * par_size + z)
        for z in range(planes)
        for m in range(2)
        for p in range(par_size)
        if p != z
    ]
    packed = total.reshape(rows * 2 * rows // LANES, LANES)
    added = lax.ppermute(packed, AXES, mirror).reshape(rows, 2 * rows)
    away = lax.dynamic_slice_in_dim(total, (1 - member) * rows, rows, 1)
    kept = lax.dynamic_slice_in_dim(total, member * rows, rows, 1)
    got = lax.ppermute(away, "ex", swap)
    return in_order(kept, got).T + added


def solution(mesh):
    return jax.shard_map(
        shards, mesh=mesh, in_specs=(P("ex", "par"),), out_specs=P("ex", "par"), check_vma=False
    )
```

```python
import jax
import jax.numpy as jnp
from jax import lax
from jax.sharding import PartitionSpec as P

AXES = ("ex", "par")
CHUNKS = 2


def tile_of(rows_a, rows_b):
    return lax.dot_general(
        rows_a, rows_b, (((1,), (1,)), ((), ())), preferred_element_type=jnp.float32
    )


def shards(jacobian):
    ex_size, par_size = lax.axis_size("ex"), lax.axis_size("par")
    planes = ex_size // 2
    half = planes // 2
    position, column = lax.axis_index("ex"), lax.axis_index("par")
    plane, member, core = position // 2, position % 2, column % 2
    way = 1 - 2 * core
    rows, cols = jacobian.shape
    width = cols // CHUNKS
    swap = [(i, i ^ 1) for i in range(ex_size)]
    onward = [
        (i * par_size + p, ((i + (2 if p % 2 == 0 else -2)) % ex_size) * par_size + p)
        for i in range(ex_size)
        for p in range(par_size)
    ]

    def in_order(block_a, block_b):
        return jnp.where(
            member == 0,
            jnp.concatenate([block_a, block_b], 0),
            jnp.concatenate([block_b, block_a], 0),
        )

    def hop(block):
        return lax.ppermute(block, AXES, onward)

    strip = jnp.zeros((planes, rows, 2 * rows), jnp.bfloat16)

    def slot_of(place):
        return place % 2 * (par_size // 2) + place // 2

    def put(strip, travel, held, where):
        tile = sum(tile_of(block, block_held) for block, block_held in zip(travel, held))
        return lax.dynamic_update_slice_in_dim(
            strip, tile.astype(jnp.bfloat16)[None], slot_of(jnp.mod(where, planes)), 0
        )

    mine = [lax.slice_in_dim(jacobian, c * width, (c + 1) * width, axis=1) for c in range(CHUNKS)]
    own = [in_order(block, lax.ppermute(block, "ex", swap)) for block in mine]
    travel = list(mine)
    strip = put(strip, travel, own, plane)
    for step in range(1, half):
        travel = [hop(block) for block in travel]
        strip = put(strip, travel, own, plane - way * step)

    def side_of(block, side):
        return lax.dynamic_slice_in_dim(block, side * (width // 2), width // 2, 1)

    theirs_side = jnp.mod(plane + way, planes) // half
    travel = [hop(side_of(block, theirs_side)) for block in travel]
    held = [side_of(block, plane // half) for block in own]
    strip = put(strip, travel, held, plane + half)

    by_slot = sorted(range(par_size), key=slot_of)
    groups = [[e * par_size + p for p in by_slot] for e in range(ex_size)]
    parts = lax.all_to_all(strip, AXES, 0, 0, axis_index_groups=groups, tiled=True)
    total = jnp.sum(parts.astype(jnp.float32), axis=0)
    mirror = [
        ((2 * z + m) * par_size + p, (2 * p + m) * par_size + z)
        for z in range(planes)
        for m in range(2)
        for p in range(par_size)
        if p != z
    ]
    added = lax.ppermute(total, AXES, mirror)
    away = lax.dynamic_slice_in_dim(total, (1 - member) * rows, rows, 1)
    kept = lax.dynamic_slice_in_dim(total, member * rows, rows, 1)
    got = lax.ppermute(away, "ex", swap)
    return in_order(kept, got).T + added


def solution(mesh):
    return jax.shard_map(
        shards, mesh=mesh, in_specs=(P("ex", "par"),), out_specs=P("ex", "par"), check_vma=False
    )
```
